256 devices in a mesh: expert: 32 (over y, z), dp: 8 (over x, core).
Axes of the slice: x: 4, y: 4, z: 8, core: 2. Of those that a mesh axis runs over, the one named last changes fastest.
Arguments:
- tokens: bfloat16 [32768, 7168], P(('expert', 'dp')), may hold values from -16 to 16
- norm_gain: float32 [7168], replicated, may hold values from 0.1 to 1.9
- routing: int32 [32768, 1], P(('expert', 'dp')), may hold values from 0 to 31; in each aligned block of 128 rows (0 to 127, 128 to 255, ...) at most 6 rows name the same one
- route_gate: float32 [32768], P(('expert', 'dp')), may hold values from 0.2 to 2
- gate_weight: bfloat16 [32, 7168, 1024], P('expert', 'dp'), may hold values from -0.0625 to 0.0625
- up_weight: bfloat16 [32, 7168, 1024], P('expert', 'dp'), may hold values from -0.0625 to 0.0625
- down_weight: bfloat16 [32, 1024, 7168], P('expert', None, 'dp'), may hold values from -0.1875 to 0.1875
- final_gain: float32 [7168], replicated, may hold values from 0.1 to 1.9
- unembed: bfloat16 [65536, 7168], P(('expert', 'dp')), may hold values from -16 to 16
- targets: int32 [512], P(('expert', 'dp')), may hold values from 0 to 65535
Outputs:
- layer_out: bfloat16 [32768, 7168], P(('expert', 'dp'))
- log_probs: float32 [512], replicated
The draws below stay inside these ranges and needn't reach their ends.
Inputs may be any that keep to these rules, and one draw needn't show every extreme that they name: `routing`: in each block of 128 consecutive tokens (the tokens of one device) no expert is named by more than 6 tokens.
All inputs are finite; a program needn't handle non-finite values.
Results may differ from the reference program's by a relative error of at most 0.023.
Values may be sent and summed in bfloat16 or wider, within the bound.
A program may use at most 128 MiB of HBM per device.

```python
import math
import jax
import jax.numpy as jnp
import numpy as np
from jax import lax

D = 7168
FW = 1024
VOC_DEV = 256
TOK_DEV = 128
LP_DEV = 2
EXPERTS_LIVE = 32
CAP = 6
TOKENS = 32768
LP_TOKENS = 512
VOCAB = 65536
N_DP = 8
DEVICES = 256


def draw_tokens(key, part):
    key_base, key_rows, key_columns = jax.random.split(key, 3)
    sample = jax.random.normal(key_base, (TOKENS, D), jnp.float32)
    row_scale = jnp.exp(jax.random.uniform(key_rows, (TOKENS, 1), jnp.float32, -1.15, 1.15))
    column_scale = jnp.exp(jax.random.uniform(key_columns, (1, D), jnp.float32, -0.6, 0.6))
    return jnp.clip(sample * row_scale * column_scale, -16.0, 16.0).astype(jnp.bfloat16)


def draw_unembed(key, part):
    scale = 3.0 / math.sqrt(D)
    sample = jnp.clip(jax.random.normal(key, (VOCAB, D), jnp.float32), -5.0, 5.0) * scale
    return jnp.clip(sample, -16.0, 16.0).astype(jnp.bfloat16)


def draw_targets(key, part):
    key = jax.random.fold_in(key, 5)
    key_shift, key_offset, key_entry = jax.random.split(key, 3)
    row_ids = jnp.arange(LP_TOKENS, dtype=jnp.int32)
    owner = row_ids // LP_DEV
    shift_value = jax.random.randint(key_shift, (), 0, 3, dtype=jnp.int32)
    kind_value = (row_ids + shift_value) % 3
    free_offset = jax.random.randint(key_offset, (LP_TOKENS,), 0, DEVICES, dtype=jnp.int32)
    offset = jnp.where(kind_value == 0, DEVICES // 2, jnp.where(kind_value == 1, 1, free_offset))
    shard = (owner + offset) % DEVICES
    entry = jax.random.randint(key_entry, (LP_TOKENS,), 0, VOC_DEV, dtype=jnp.int32)
    return (shard * VOC_DEV + entry).astype(jnp.int32)


def level_of(key, dims, cuts, smallest, largest):
    factor_of = 1.0
    for position, blocks in cuts:
        draws = jax.random.uniform(jax.random.fold_in(jax.random.fold_in(key, 6), position), (blocks,), jnp.float32, smallest / len(cuts), largest / len(cuts))
        factor_of = factor_of * jnp.repeat(jnp.exp(draws), dims[position] // blocks).reshape((-1,) + (1,) * (len(dims) - 1 - position))
    return factor_of


def deal_out(key, own, number, rows, count, top, limit, skew):
    order = jax.random.permutation(key, count)
    packed, common = portions_of(count, rows * top, limit, skew, True), portions_of(count, rows * top, limit, skew, False)
    places = jnp.arange(count)

    def named(sizes, rotation):
        used = int((sizes > 0).sum())
        fixed = max(1, used // 4)
        passed = fixed + (places - fixed + rotation * (used - fixed)) % max(1, count - fixed)
        return jnp.zeros((count,), jnp.int32).at[order[jnp.where(places < fixed, places, passed)]].set(jnp.asarray(sizes, jnp.int32))

    sizes = jnp.where(number % 4 == 0, named(packed, number // 4), named(common, number - number // 4 - 1))
    mixed = jax.random.permutation(jax.random.fold_in(own, 3), count)
    giver, sink = mixed[0:count // 2 * 2:2], mixed[1:count // 2 * 2:2]
    margin = jnp.minimum(sizes[giver] - 1, limit - sizes[sink]) // 2
    margin = jnp.where((giver == order[0]) | (sink == order[0]) | (sizes[sink] == 0), 0, jnp.maximum(margin, 0))
    passed = jax.random.randint(jax.random.fold_in(own, 4), (count // 2,), 0, 1 << 20) % (margin + 1)
    sizes = sizes.at[giver].add(-passed).at[sink].add(passed)
    labels = jnp.searchsorted(jnp.cumsum(sizes), jnp.arange(rows * top), side="right").astype(jnp.int32)
    table = labels.reshape(top, rows).T
    table = table[jax.random.permutation(jax.random.fold_in(own, 1), rows)]
    rotation = jax.random.randint(jax.random.fold_in(own, 2), (rows, 1), 0, top)
    return jnp.take_along_axis(table, (jnp.arange(top)[None, :] + rotation) % top, axis=1)


def portions_of(amount, total, reach, slope, full):
    portions = [(1 << 20) // math.isqrt(standing ** slope) + 1 for standing in range(1, amount + 1)]
    largest = reach if full else min(reach, max(-(-total // amount), total * portions[0] // sum(portions)))
    least = 1 if total - largest >= amount - 1 else 0
    holding, spare = [largest] + [least] * (amount - 1), total - largest - least * (amount - 1)
    while spare > 0:
        movable = [i for i in range(1, amount) if holding[i] < largest] or [i for i in range(1, amount) if holding[i] < reach]
        whole, budget = sum([portions[i] for i in movable]), spare
        for i in movable:
            addition = min(reach - holding[i], max(1, budget * portions[i] // whole), spare)
            holding[i] = holding[i] + addition
            spare = spare - addition
    return np.array(holding)


def noise(rng, dims, deviation, limit, shards=(), kind=jnp.bfloat16):
    result = deviation * jax.random.normal(rng, dims, jnp.float32)
    if shards:
        result = result * level_of(rng, dims, shards, -0.22, 0.18)
    return jnp.clip(result, -limit, limit).astype(kind)


def setup_inputs(seed: int = 0) -> dict:
    key_of = jax.random.split(jax.random.key(seed), 11)
    tokens = draw_tokens(jax.random.fold_in(key_of[10], 71), 0)
    norm_gain = jnp.clip(1.0 + 0.18 * jax.random.normal(key_of[1], (D,), jnp.float32), 0.1, 1.9)
    routing_keys = jax.random.split(jax.random.fold_in(key_of[2], 1), TOKENS // TOK_DEV)
    routing_turns = jax.random.permutation(jax.random.fold_in(key_of[2], 3), TOKENS // TOK_DEV)
    routing = jax.vmap(lambda own, number: deal_out(jax.random.fold_in(key_of[2], 2), own, number, TOK_DEV, EXPERTS_LIVE, 1, CAP, 2))(routing_keys, routing_turns).reshape((TOKENS, 1))
    route_gate = jnp.clip(0.2 + 1.8 * jax.random.uniform(key_of[3], (TOKENS,), jnp.float32) ** level_of(key_of[3], (TOKENS,), ((0, 256),), -0.2, 0.2), 0.2, 2.0)
    gate_weight = noise(key_of[4], (EXPERTS_LIVE, D, FW), D ** -0.5, 0.0625, ((0, 32), (1, 8)))
    up_weight = noise(key_of[5], (EXPERTS_LIVE, D, FW), D ** -0.5, 0.0625, ((0, 32), (1, 8)))
    down_weight = noise(key_of[6], (EXPERTS_LIVE, FW, D), FW ** -0.5, 0.1875, ((0, 32), (2, 8)))
    final_gain = jnp.clip(1.0 + 0.18 * jax.random.normal(key_of[7], (D,), jnp.float32), 0.1, 1.9)
    unembed = draw_unembed(jax.random.fold_in(key_of[10], 71), 0)
    targets = draw_targets(jax.random.fold_in(key_of[10], 71), 0)
    return dict(tokens=tokens, norm_gain=norm_gain, routing=routing, route_gate=route_gate, gate_weight=gate_weight, up_weight=up_weight, down_weight=down_weight, final_gain=final_gain, unembed=unembed, targets=targets)


EPSILON = 1e-06

def rms_scale(values, scale_gain):
    wide = values.astype(jnp.float32)
    mean_sq = lax.optimization_barrier(jnp.mean(wide * wide, axis=-1, keepdims=True))
    return (wide * lax.rsqrt(mean_sq + EPSILON) * scale_gain.astype(jnp.float32)).astype(jnp.bfloat16)

def block_sum(values, weight):
    pieces = values.reshape(values.shape[0], N_DP, -1).astype(jnp.float32)
    weight_parts = weight.reshape(N_DP, -1, weight.shape[1]).astype(jnp.float32)
    partial_sums = jnp.einsum('rkd,kdf->krf', pieces, weight_parts).astype(jnp.bfloat16)
    return lax.optimization_barrier(jnp.sum(partial_sums.astype(jnp.float32), axis=0))

def run_expert(operands):
    values, gate_w, up_w, down_w = operands
    gate = block_sum(values, gate_w)
    up_part = block_sum(values, up_w)
    hidden = (jax.nn.silu(gate) * up_part).astype(jnp.bfloat16)
    return jnp.dot(hidden, down_w, preferred_element_type=jnp.float32).astype(jnp.bfloat16)

def reference(tokens, norm_gain, routing, route_gate, gate_weight, up_weight, down_weight, final_gain, unembed, targets):
    normed = rms_scale(tokens, norm_gain)
    blocks = TOKENS // TOK_DEV
    expert = routing[:, 0].astype(jnp.int32)
    grid = expert.reshape(blocks, TOK_DEV)
    onehot = (grid[:, :, None] == jnp.arange(EXPERTS_LIVE, dtype=jnp.int32)[None, None, :]).astype(jnp.int32)
    before = jnp.cumsum(onehot, axis=1) - onehot
    slot_rank = lax.optimization_barrier(jnp.sum(before * onehot, axis=2)).reshape(-1)
    owner = jnp.arange(TOKENS, dtype=jnp.int32) // TOK_DEV
    stride = blocks * CAP
    slot_index = (expert * stride + owner * CAP + slot_rank).astype(jnp.int32)
    buffer = jnp.zeros((EXPERTS_LIVE * stride, D), jnp.bfloat16).at[slot_index].set(normed)
    buffer = buffer.reshape(EXPERTS_LIVE, stride, D)
    outputs = lax.map(run_expert, (buffer, gate_weight, up_weight, down_weight)).reshape(-1, D)
    picked_rows = outputs[slot_index].astype(jnp.float32)
    layer_out = (tokens.astype(jnp.float32) + route_gate[:, None] * picked_rows).astype(jnp.bfloat16)
    scored = layer_out.reshape(blocks, TOK_DEV, D)[:, :LP_DEV].reshape(-1, D)
    final = rms_scale(scored, final_gain)
    logits = jnp.dot(final, unembed.T, preferred_element_type=jnp.float32)
    row_top = lax.optimization_barrier(jnp.max(logits, axis=1))
    row_total = lax.optimization_barrier(jnp.sum(jnp.exp(logits - row_top[:, None]), axis=1))
    target_logit = jnp.take_along_axis(logits, targets[:, None].astype(jnp.int32), axis=1)[:, 0]
    log_probs = target_logit - (row_top + jnp.log(row_total))
    return (layer_out, log_probs)
```

```python
import functools

import jax
import jax.numpy as jnp
from jax import lax
from jax.experimental import pallas as pl
from jax.experimental.pallas import tpu as pltpu
from jax.sharding import PartitionSpec as P

MESH = pl.DeviceIdType.MESH
NY, NZ, NX = 4, 8, 4
EPSILON = 1e-06
CHUNKS = 3
SLOTS = 2
VMEM_LIMIT = 62 * 2**20

X, Z, CP, XP, HX, HC, R, T = (3 * i for i in range(8))
TS, IN, FZ, SQ, IZ, IY, FX, FYA, FYB, FC1, FC2, STZ, STY, STD = range(24, 38)
SEMS = 38

F32, BF16 = jnp.float32, jnp.bfloat16


def iota(shape, dim):
    return lax.broadcasted_iota(jnp.int32, shape, dim)


def dot(a, b):
    return jnp.dot(a, b, preferred_element_type=F32)


def kernel(
    tok_h, gain_ref, rc_ref, rr_ref, rg_ref, tg_ref, wg_h, wu_h, wd_h, fg_ref, un_h,
    out_h, lp_ref,
    tok, nb, w, wd, un, pm, um, q, qt, xs, xr, zs, za, part, crecv, xrecv, hid, rb, g,
    ts, tr, t16, ins, inr, info, sq, fs, acc, st, stz, sty, std, ssem, rsem, lsem, osem,
):
    dp = 2 * NX
    experts = NY * NZ
    e, d = lax.axis_index("expert"), lax.axis_index("dp")
    y, z = lax.div(e, NZ), lax.rem(e, NZ)
    x, c = lax.div(d, 2), lax.rem(d, 2)
    sib = d + 1 - 2 * c
    rows_tok, width = tok.shape
    blk = width // dp
    lanes = xs.shape[2]
    msg = dp * SLOTS
    rows = experts * msg
    he = experts // 2
    own = rows // dp
    units = wd.shape[0]

    def send(src, dst, idx, to):
        pltpu.make_async_remote_copy(
            src_ref=src, dst_ref=dst, send_sem=ssem.at[idx], recv_sem=rsem.at[idx],
            device_id=to, device_id_type=MESH,
        ).start()

    def landed(ref, idx):
        pltpu.make_async_copy(ref, ref, rsem.at[idx]).wait()

    def sent(ref, idx):
        pltpu.make_async_copy(ref, ref, ssem.at[idx]).wait()

    def loop(lo, hi, body):
        def step(i, carry):
            body(i)
            return carry
        lax.fori_loop(lo, hi, step, 0)

    def expert_at(i):
        dz, dy = lax.div(i, NY), lax.rem(i, NY)
        return lax.rem(y + dy, NY) * NZ + lax.rem(z + dz, NZ)

    def dp_at(i):
        return lax.rem(d + i, dp)

    def columns(k):
        return pl.ds(pl.multiple_of(k * blk, 128), blk)

    loads = [
        pltpu.make_async_copy(src, dst, lsem.at[i])
        for i, (src, dst) in enumerate([
            (tok_h, tok), (wg_h.at[0], w.at[:, pl.ds(0, units)]),
            (wu_h.at[0], w.at[:, pl.ds(units, units)]), (wd_h.at[0], wd), (un_h, un),
        ])
    ]
    for load in loads:
        load.start()
    barrier = pltpu.get_barrier_semaphore()

    def greet_dp(i):
        pl.semaphore_signal(barrier, inc=1, device_id=(e, dp_at(i)), device_id_type=MESH)

    def greet_expert(i):
        pl.semaphore_signal(barrier, inc=1, device_id=(expert_at(i), d), device_id_type=MESH)

    loop(1, experts, greet_expert)
    loop(1, dp, greet_dp)

    ec, er = rc_ref[...].astype(F32), rr_ref[...].astype(F32)
    same = ec == er
    before, after = iota(same.shape, 0), iota(same.shape, 1)
    rank_row = jnp.sum(jnp.where(same & (before < after), 1.0, 0.0), axis=0, keepdims=True)
    rank_col = jnp.sum(jnp.where(same & (after < before), 1.0, 0.0), axis=1, keepdims=True)

    def slot_of(rank, expert):
        chunk = jnp.floor(rank * (1.0 / SLOTS))
        return chunk * lanes + expert * SLOTS + (rank - chunk * SLOTS)

    pm[...] = jnp.where(iota(pm.shape, 0).astype(F32) == slot_of(rank_row, er), 1.0, 0.0).astype(BF16)
    um[...] = jnp.where(iota(um.shape, 1).astype(F32) == slot_of(rank_col, ec), 1.0, 0.0).astype(BF16)

    lane = iota((msg, 128), 1)
    row = iota((msg, 128), 0)
    base = jnp.where(
        lane == 1, ec[:msg] * msg + (d * SLOTS).astype(F32) + rank_col[:msg],
        jnp.where(lane == 2, rg_ref[0:msg, :], 0.0),
    )
    first = jnp.where(lane == 0, tg_ref[0].astype(F32), base[0:1])
    second = jnp.where(lane == 0, tg_ref[1].astype(F32), base[1:2])
    ins[...] = jnp.where(row == 2 * d, first, jnp.where(row == 2 * d + 1, second, 0.0))
    inr[d] = ins[...]

    loads[0].wait()
    tile = min(16, rows_tok)

    def norm(i):
        at = pl.ds(pl.multiple_of(i * tile, tile), tile)
        wide = tok[at, :].astype(F32)
        mean_sq = jnp.mean(wide * wide, axis=-1, keepdims=True)
        nb[at, :] = (wide * lax.rsqrt(mean_sq + EPSILON) * gain_ref[...]).astype(BF16)

    loop(0, rows_tok // tile, norm)

    def place(ch):
        def body(k):
            xs[ch, k] = dot(pm[ch * lanes:(ch + 1) * lanes, :], nb[:, columns(k)]).astype(BF16)
        loop(0, dp, body)
        xr[ch, d] = xs[ch, d]

    def place_send(ch):
        def body(i):
            send(xs.at[ch, dp_at(i)], xr.at[ch, d], X + ch, (e, dp_at(i)))
        loop(1, dp, body)

    place(0)
    pl.semaphore_wait(barrier, experts - 1 + dp - 1)
    place_send(0)

    def scored_tokens(k):
        r16 = iota((msg, blk), 0)
        top = tok[0:msg, columns(k)].astype(F32)
        ts[k] = jnp.where(r16 == 2 * d, top[0:1], jnp.where(r16 == 2 * d + 1, top[1:2], 0.0)).astype(BF16)

    loop(0, dp, scored_tokens)
    tr[d] = ts[d]
    loop(1, dp, lambda i: send(ins, inr.at[d], IN, (e, dp_at(i))))
    loop(1, dp, lambda i: send(ts.at[dp_at(i)], tr.at[d], TS, (e, dp_at(i))))
    for ch in range(1, CHUNKS):
        place(ch)
        place_send(ch)

    part_rows = rows // 8

    def permutations(i):
        at = pl.ds(pl.multiple_of(i * part_rows, part_rows), part_rows)
        a = iota((part_rows, rows), 0) + i * part_rows
        b = iota((part_rows, rows), 1)
        ex, dev, slot = lax.div(a, msg), lax.rem(lax.div(a, SLOTS), dp), lax.rem(a, SLOTS)
        q[at, :] = jnp.where(b == dev * lanes + ex * SLOTS + slot, 1.0, 0.0).astype(BF16)
        ex, dev = lax.rem(lax.div(a, SLOTS), experts), lax.div(a, lanes)
        qt[at, :] = jnp.where(b == ex * msg + dev * SLOTS + slot, 1.0, 0.0).astype(BF16)

    loop(0, 8, permutations)

    def dispatch(ch):
        landed(xr.at[ch, pl.ds(0, dp - 1)], X + ch)

        def body(i):
            at = pl.ds(pl.multiple_of(i * (rows // 2), rows // 2), rows // 2)
            moved = dot(q[at, :], xr[ch].reshape(rows, blk)).astype(BF16)
            zs[ch, pl.ds(i * he, he)] = moved.reshape(he, msg, blk)
        loop(0, 2, body)
        za[ch, e] = zs[ch, e]
        loop(1, experts, lambda i: send(zs.at[ch, expert_at(i)], za.at[ch, e], Z + ch, (expert_at(i), d)))

    dispatch(0)
    for load in loads[1:]:
        load.wait()
    landed(inr.at[pl.ds(0, dp - 1)], IN)
    landed(tr.at[pl.ds(0, dp - 1)], TS)
    total = inr[0]
    tokens16 = tr[0].astype(F32)
    for k in range(1, dp):
        total = total + inr[k]
        tokens16 = tokens16 + tr[k].astype(F32)
    ins_total = total
    t16[...] = tokens16
    dispatch(1)
    dispatch(2)

    def gate_up(ch):
        landed(za.at[ch, pl.ds(0, experts - 1)], Z + ch)
        step = min(256, units)

        def half(p):
            def body(n):
                at = pl.ds(pl.multiple_of(n * step, step), step)
                values = za[ch, pl.ds(p * he, he)].reshape(he * msg, blk)
                part[ch, p, :, at] = dot(values, w[:, at]).astype(BF16)
            loop(0, 2 * units // step, body)

        half(1 - c)
        send(part.at[ch, 1 - c], crecv.at[ch], CP + ch, (e, sib))
        half(c)
        landed(crecv.at[ch], CP + ch)

        def add(i):
            to = lax.rem(x + i, NX)
            at = pl.ds(pl.multiple_of(to * own, own), own)
            part[ch, c, at, :] = (part[ch, c, at, :].astype(F32) + crecv[ch, at, :].astype(F32)).astype(BF16)
            return to, at

        def body(i):
            to, at = add(i)
            send(part.at[ch, c, at, :], xrecv.at[ch, i - 1], XP + ch, (e, 2 * to + c))
        loop(1, NX, body)
        add(0)

    def activate(ch):
        landed(xrecv.at[ch], XP + ch)
        at = pl.ds(pl.multiple_of(x * own, own), own)
        summed = part[ch, c, at, :].astype(F32)
        for i in range(NX - 1):
            summed = summed + xrecv[ch, i].astype(F32)
        gate, up = summed[:, :units], summed[:, units:]
        hid[ch, c, x] = (gate / (1.0 + jnp.exp(-gate)) * up).astype(BF16)
        loop(1, NX, lambda i: send(hid.at[ch, c, x], hid.at[ch, c, x], HX + ch, (e, 2 * lax.rem(x + i, NX) + c)))

    def share(ch):
        landed(hid.at[ch, c, pl.ds(0, NX - 1)], HX + ch)
        send(hid.at[ch, c], hid.at[ch, c], HC + ch, (e, sib))

    def down(ch):
        sent(zs.at[ch, pl.ds(0, experts - 1)], Z + ch)

        def body(i):
            p = c + i - 2 * c * i

            @pl.when(i == 1)
            def _():
                landed(hid.at[ch, c], HC + ch)

            result = dot(hid[ch, p].reshape(he * msg, units), wd[...]).astype(BF16)
            zs[ch, pl.ds(p * he, he)] = result.reshape(he, msg, blk)

            def give(j):
                to = p * he + lax.rem(j + e, he)

                @pl.when(to != e)
                def _():
                    send(zs.at[ch, to], rb.at[ch, e], R + ch, (to, d))
            loop(0, he, give)
        loop(0, 2, body)
        rb[ch, e] = zs[ch, e]

    def back(ch):
        landed(rb.at[ch, pl.ds(0, experts - 1)], R + ch)

    def home(ch):
        sent(xs.at[ch, pl.ds(0, dp - 1)], X + ch)

        def body(i):
            at = pl.ds(pl.multiple_of(i * (rows // 2), rows // 2), rows // 2)
            moved = dot(qt[at, :], rb[ch].reshape(rows, blk)).astype(BF16)
            xs[ch, pl.ds(i * (dp // 2), dp // 2)] = moved.reshape(dp // 2, lanes, blk)
        loop(0, 2, body)
        g[d, ch * lanes:(ch + 1) * lanes, :] = xs[ch, d]
        loop(1, dp, lambda i: send(
            xs.at[ch, dp_at(i)], g.at[d, pl.ds(ch * lanes, lanes), :], T + ch, (e, dp_at(i))))

    def score_rows():
        slot, scale = ins_total[:, 1:2], ins_total[:, 2:3]
        pick = jnp.where(iota((msg, rows), 1).astype(F32) == slot, 1.0, 0.0).astype(BF16)
        picked = dot(pick, rb[0].reshape(rows, blk))
        layer = (t16[...] + scale * picked).astype(BF16).astype(F32)
        fs[c, y, x, z] = (layer * fg_ref[:, columns(d)]).astype(BF16)
        loop(1, NZ, lambda i: send(
            fs.at[c, y, x, z], fs.at[c, y, x, z], FZ, (y * NZ + lax.rem(z + i, NZ), d)))
        squares = jnp.sum(layer * layer, axis=-1, keepdims=True)
        sq[d] = jnp.broadcast_to(squares, (msg, 128))
        loop(1, dp, lambda i: send(sq.at[d], sq.at[d], SQ, (e, dp_at(i))))

    def score_info():
        landed(sq.at[pl.ds(0, dp - 1)], SQ)
        squares = sq[0]
        for k in range(1, dp):
            squares = squares + sq[k]
        info[y, z] = jnp.where(lane == 1, squares, ins_total)
        loop(1, NZ, lambda i: send(info.at[y, z], info.at[y, z], IZ, (y * NZ + lax.rem(z + i, NZ), d)))

    def to_y(i):
        return (lax.rem(y + i, NY) * NZ + z, d)

    def score_x():
        landed(fs.at[c, y, x, pl.ds(0, NZ - 1)], FZ)
        piece = fs.at[c, y, x]
        loop(1, NX, lambda i: send(piece, piece, FX, (e, 2 * lax.rem(x + i, NX) + c)))
        loop(1, NY, lambda i: send(piece, piece, FYA, to_y(i)))
        landed(info.at[y, pl.ds(0, NZ - 1)], IZ)
        loop(1, NY, lambda i: send(info.at[y], info.at[y], IY, to_y(i)))

    def score_y():
        landed(fs.at[c, y, pl.ds(0, NX - 1)], FX)

        def body(j):
            piece = fs.at[c, y, lax.rem(x + j, NX)]
            loop(1, NY, lambda i: send(piece, piece, FYB, to_y(i)))
        loop(1, NX, body)
        send(fs.at[c, y], fs.at[c, y], FC1, (e, sib))

    def score_core():
        landed(fs.at[c, pl.ds(0, NY - 1), 0], FYA)
        landed(fs.at[c, pl.ds(0, NY - 1), pl.ds(0, NX - 1)], FYB)

        def body(i):
            piece = fs.at[c, lax.rem(y + i, NY)]
            send(piece, piece, FC2, (e, sib))
        loop(1, NY, body)

    def logits_half(p, start):
        def body(i):
            values = fs[p, :, i].reshape(rows, blk)
            product = lax.dot_general(
                un[:, columns(2 * i + p)], values, (((1,), (1,)), ((), ())), preferred_element_type=F32)
            acc[...] += product
        if start:
            acc[...] = jnp.zeros_like(acc)
        loop(0, NX, body)

    def combine(ref, n):
        top = ref[0, 0:1]
        for k in range(1, n):
            top = jnp.maximum(top, ref[k, 0:1])
        total = jnp.zeros_like(top)
        picked = jnp.zeros_like(top)
        for k in range(n):
            total = total + ref[k, 1:2] * jnp.exp(ref[k, 0:1] - top)
            picked = picked + ref[k, 2:3]
        return top, total, picked

    def put(ref, at, stats):
        r8 = iota(ref.shape[1:], 0)
        ref[at] = jnp.where(r8 == 0, stats[0], jnp.where(r8 == 1, stats[1], jnp.where(r8 == 2, stats[2], 0.0)))

    def score_logits():
        logits_half(c, True)
        landed(fs.at[c, 0], FC1)
        landed(fs.at[c, pl.ds(0, NY - 1)], FC2)
        logits_half(1 - c, False)
        landed(info.at[pl.ds(0, NY - 1)], IY)
        known = info[...].reshape(rows, 128).T
        target, squares = known[0:1], known[1:2]
        logits = acc[...] * lax.rsqrt(squares * (1.0 / width) + EPSILON)
        top = jnp.max(logits, axis=0, keepdims=True)
        total = jnp.sum(jnp.exp(logits - top), axis=0, keepdims=True)
        entry = iota(logits.shape, 0) + (e * dp + d) * logits.shape[0]
        picked = jnp.sum(jnp.where(entry.astype(F32) == target, logits, 0.0), axis=0, keepdims=True)
        put(stz, z, (top, total, picked))
        loop(1, NZ, lambda i: send(stz.at[z], stz.at[z], STZ, (y * NZ + lax.rem(z + i, NZ), d)))

    def score_stats_y():
        landed(stz.at[pl.ds(0, NZ - 1)], STZ)
        put(sty, y, combine(stz, NZ))
        loop(1, NY, lambda i: send(sty.at[y], sty.at[y], STY, to_y(i)))

    def score_stats_dp():
        landed(sty.at[pl.ds(0, NY - 1)], STY)
        put(std, d, combine(sty, NY))
        loop(1, dp, lambda i: send(std.at[d], std.at[d], STD, (e, dp_at(i))))

    def score_end():
        landed(std.at[pl.ds(0, dp - 1)], STD)
        top, total, picked = combine(std, dp)
        lp_ref[...] = picked - (top + jnp.log(total))

    def finish():
        for ch in range(CHUNKS):
            landed(g.at[pl.ds(0, dp - 1), pl.ds(0, lanes), :], T + ch)

        def body(k):
            at = columns(k)
            picked = dot(um[...], g[k])
            tok[:, at] = (tok[:, at].astype(F32) + rg_ref[...] * picked).astype(BF16)
            pltpu.make_async_copy(tok.at[:, at], out_h.at[:, at], osem).start()
        loop(0, dp, body)

    gate_up(0)
    activate(0)
    gate_up(1)
    share(0)
    down(0)
    activate(1)
    share(1)
    down(1)
    gate_up(2)
    back(0)
    score_rows()
    home(0)
    score_info()
    score_x()
    activate(2)
    share(2)
    score_y()
    down(2)
    back(1)
    home(1)
    back(2)
    home(2)
    score_core()
    score_logits()
    score_stats_y()
    finish()
    score_stats_dp()
    score_end()

    pltpu.make_async_copy(tok, out_h, osem).wait()
    for ch in range(CHUNKS):
        sent(part.at[ch, 0], CP + ch)
        sent(xrecv.at[ch], XP + ch)
        sent(hid.at[ch, 0, pl.ds(0, NX - 1)], HX + ch)
        sent(hid.at[ch, 0], HC + ch)
        sent(zs.at[ch, pl.ds(0, experts - 1)], R + ch)
        sent(xs.at[ch, pl.ds(0, dp - 1)], T + ch)
    sent(inr.at[pl.ds(0, dp - 1)], IN)
    sent(tr.at[pl.ds(0, dp - 1)], TS)
    sent(fs.at[0, 0, 0, pl.ds(0, NZ - 1)], FZ)
    sent(sq.at[pl.ds(0, dp - 1)], SQ)
    sent(info.at[0, pl.ds(0, NZ - 1)], IZ)
    sent(info.at[pl.ds(0, NY - 1)], IY)
    sent(fs.at[0, 0, pl.ds(0, NX - 1)], FX)
    sent(fs.at[0, pl.ds(0, NY - 1), 0], FYA)
    sent(fs.at[0, pl.ds(0, NY - 1), pl.ds(0, NX - 1)], FYB)
    sent(fs.at[0, 0], FC1)
    sent(fs.at[0, pl.ds(0, NY - 1)], FC2)
    sent(stz.at[pl.ds(0, NZ - 1)], STZ)
    sent(sty.at[pl.ds(0, NY - 1)], STY)
    sent(std.at[pl.ds(0, dp - 1)], STD)


def local(
    tokens, norm_gain, routing, route_gate, gate_weight, up_weight, down_weight,
    final_gain, unembed, targets,
):
    rows_tok, width = tokens.shape
    dp, experts = 2 * NX, NY * NZ
    blk, units, vocab = width // dp, up_weight.shape[2], unembed.shape[0]
    lanes, msg = experts * SLOTS, dp * SLOTS
    rows = experts * msg
    own = rows // dp
    vmem = pl.BlockSpec(memory_space=pltpu.VMEM)
    hbm = pl.BlockSpec(memory_space=pl.ANY)
    smem = pl.BlockSpec(memory_space=pltpu.SMEM)
    layer_out, log_probs = pl.pallas_call(
        kernel,
        out_shape=(
            jax.ShapeDtypeStruct((rows_tok, width), BF16),
            jax.ShapeDtypeStruct((1, rows), F32),
        ),
        in_specs=[hbm, vmem, vmem, vmem, vmem, smem, hbm, hbm, hbm, vmem, hbm],
        out_specs=(hbm, vmem),
        scratch_shapes=[
            pltpu.VMEM((rows_tok, width), BF16),
            pltpu.VMEM((rows_tok, width), BF16),
            pltpu.VMEM((blk, 2 * units), BF16),
            pltpu.VMEM((units, blk), BF16),
            pltpu.VMEM((vocab, width), BF16),
            pltpu.VMEM((CHUNKS * lanes, rows_tok), BF16),
            pltpu.VMEM((rows_tok, CHUNKS * lanes), BF16),
            pltpu.VMEM((rows, rows), BF16),
            pltpu.VMEM((rows, rows), BF16),
            pltpu.VMEM((CHUNKS, dp, lanes, blk), BF16),
            pltpu.VMEM((CHUNKS, dp, lanes, blk), BF16),
            pltpu.VMEM((CHUNKS, experts, msg, blk), BF16),
            pltpu.VMEM((CHUNKS, experts, msg, blk), BF16),
            pltpu.VMEM((CHUNKS, 2, rows // 2, 2 * units), BF16),
            pltpu.VMEM((CHUNKS, rows // 2, 2 * units), BF16),
            pltpu.VMEM((CHUNKS, NX - 1, own, 2 * units), BF16),
            pltpu.VMEM((CHUNKS, 2, NX, own, units), BF16),
            pltpu.VMEM((CHUNKS, experts, msg, blk), BF16),
            pltpu.VMEM((dp, CHUNKS * lanes, blk), BF16),
            pltpu.VMEM((dp, msg, blk), BF16),
            pltpu.VMEM((dp, msg, blk), BF16),
            pltpu.VMEM((msg, blk), F32),
            pltpu.VMEM((msg, 128), F32),
            pltpu.VMEM((dp, msg, 128), F32),
            pltpu.VMEM((NY, NZ, msg, 128), F32),
            pltpu.VMEM((dp, msg, 128), F32),
            pltpu.VMEM((2, NY, NX, NZ, msg, blk), BF16),
            pltpu.VMEM((vocab, rows), F32),
            pltpu.VMEM((8, rows), F32),
            pltpu.VMEM((NZ, 8, rows), F32),
            pltpu.VMEM((NY, 8, rows), F32),
            pltpu.VMEM((dp, 8, rows), F32),
            pltpu.SemaphoreType.DMA((SEMS,)),
            pltpu.SemaphoreType.DMA((SEMS,)),
            pltpu.SemaphoreType.DMA((5,)),
            pltpu.SemaphoreType.DMA,
        ],
        compiler_params=pltpu.CompilerParams(
            collective_id=0, has_side_effects=True, vmem_limit_bytes=VMEM_LIMIT
        ),
        name="routed_layer",
    )(
        tokens, norm_gain.reshape(1, width), routing, routing.reshape(1, rows_tok),
        route_gate.reshape(rows_tok, 1), targets, gate_weight, up_weight, down_weight,
        final_gain.reshape(1, width), unembed,
    )
    return layer_out, log_probs.reshape(rows)


def solution(mesh):
    placed = (
        P(("expert", "dp"), None),
        P(),
        P(("expert", "dp"), None),
        P(("expert", "dp")),
        P("expert", "dp", None),
        P("expert", "dp", None),
        P("expert", None, "dp"),
        P(),
        P(("expert", "dp"), None),
        P(("expert", "dp")),
    )
    return jax.shard_map(
        local,
        mesh=mesh,
        in_specs=placed,
        out_specs=(P(("expert", "dp"), None), P()),
        check_vma=False,
    )
```

```python
import functools

import jax
import jax.numpy as jnp
from jax import lax
from jax.experimental import pallas as pl
from jax.experimental.pallas import tpu as pltpu
from jax.sharding import PartitionSpec as P

MESH = pl.DeviceIdType.MESH
NY, NZ, NX = 4, 8, 4
EPSILON = 1e-06
CHUNKS = 3
SLOTS = 2
VMEM_LIMIT = 62 * 2**20

X, CP, XP, HX, HC = (6 * i for i in range(5))
Z, R, T = 30, 33, 36
TS, IN, FZ, SQ, IZ, IY, FX, FYA, FYB, FC1, FC2, STZ, STY, STD = range(39, 53)
SEMS = 53

F32, BF16 = jnp.float32, jnp.bfloat16


def iota(shape, dim):
    return lax.broadcasted_iota(jnp.int32, shape, dim)


def dot(a, b):
    return jnp.dot(a, b, preferred_element_type=F32)


def kernel(
    tok_h, gain_ref, rr_ref, rgr_ref, tg_ref, wg_h, wu_h, wd_h, fg_ref, un_h,
    out_h, lp_ref,
    rg_ref, tok, nb, w, wd, un, pm, um, q, qt, xs, xr, zs, za, part, crecv, xrecv, hid, rb, g,
    ts, tr, t16, it16, ins, inr, info, sq, fs, acc, st, stz, sty, std, ssem, rsem, lsem, osem,
):
    dp = 2 * NX
    experts = NY * NZ
    e, d = lax.axis_index("expert"), lax.axis_index("dp")
    y, z = lax.div(e, NZ), lax.rem(e, NZ)
    x, c = lax.div(d, 2), lax.rem(d, 2)
    sib = d + 1 - 2 * c
    rows_tok, width = tok.shape
    blk = width // dp
    half_lanes = xs.shape[3]
    lanes = 2 * half_lanes
    msg = dp * SLOTS
    rows = experts * msg
    he = experts // 2
    own = rows // dp
    units = wd.shape[0]
    hu = units // 2
    zh = NZ // 2
    place_me = lax.rem(z, 2) * he + y * zh + lax.div(z, 2)
    f_me, s_me = x * (1 - c) + y * c, y * (1 - c) + x * c

    def send(src, dst, idx, to):
        pltpu.make_async_remote_copy(
            src_ref=src, dst_ref=dst, send_sem=ssem.at[idx], recv_sem=rsem.at[idx],
            device_id=to, device_id_type=MESH,
        ).start()

    def landed(ref, idx):
        pltpu.make_async_copy(ref, ref, rsem.at[idx]).wait()

    pending = {}

    def later(ref, idx):
        pending[idx] = ref

    def sent(idx):
        ref = pending.pop(idx)
        pltpu.make_async_copy(ref, ref, ssem.at[idx]).wait()

    def loop(lo, hi, body):
        def step(i, carry):
            body(i)
            return carry
        lax.fori_loop(lo, hi, step, 0)

    def expert_at(i):
        dz, dy = lax.div(i, NY), lax.rem(i, NY)
        return lax.rem(y + dy, NY) * NZ + lax.rem(z + dz, NZ)

    def dp_at(i):
        return lax.rem(d + i, dp)

    def columns(k):
        return pl.ds(pl.multiple_of(k * blk, 128), blk)

    loads = [
        pltpu.make_async_copy(src, dst, lsem.at[i])
        for i, (src, dst) in enumerate([
            (tok_h, tok),
            (wg_h.at[0, :, pl.ds(0, hu)], w.at[0, :, pl.ds(0, hu)]),
            (wu_h.at[0, :, pl.ds(0, hu)], w.at[0, :, pl.ds(hu, hu)]),
            (wg_h.at[0, :, pl.ds(hu, hu)], w.at[1, :, pl.ds(0, hu)]),
            (wu_h.at[0, :, pl.ds(hu, hu)], w.at[1, :, pl.ds(hu, hu)]),
            (wd_h.at[0], wd), (un_h, un),
        ])
    ]
    for load in loads:
        load.start()
    barrier = pltpu.get_barrier_semaphore()

    def greet_dp(i):
        pl.semaphore_signal(barrier, inc=1, device_id=(e, dp_at(i)), device_id_type=MESH)

    def greet_expert(i):
        pl.semaphore_signal(barrier, inc=1, device_id=(expert_at(i), d), device_id_type=MESH)

    loop(1, experts, greet_expert)
    loop(1, dp, greet_dp)

    def column(values):
        n = values.shape[1]
        return jnp.sum(jnp.where(iota((n, n), 0) == iota((n, n), 1), values, 0.0), axis=1, keepdims=True)

    er = rr_ref[...].astype(F32)
    ec = column(er)
    rg_ref[...] = column(rgr_ref[...])
    same = ec == er
    before, after = iota(same.shape, 0), iota(same.shape, 1)
    rank_row = jnp.sum(jnp.where(same & (before < after), 1.0, 0.0), axis=0, keepdims=True)
    rank_col = jnp.sum(jnp.where(same & (after < before), 1.0, 0.0), axis=1, keepdims=True)

    def place_of(expert):
        at_y = jnp.floor(expert * (1.0 / NZ))
        at_z = expert - at_y * NZ
        half_z = jnp.floor(at_z * 0.5)
        return (at_z - 2.0 * half_z) * he + at_y * zh + half_z

    def slot_of(rank, expert):
        chunk = jnp.floor(rank * (1.0 / SLOTS))
        return chunk * lanes + place_of(expert) * SLOTS + (rank - chunk * SLOTS)

    pm[...] = jnp.where(iota(pm.shape, 0).astype(F32) == slot_of(rank_row, er), 1.0, 0.0).astype(BF16)
    um[...] = jnp.where(iota(um.shape, 1).astype(F32) == slot_of(rank_col, ec), 1.0, 0.0).astype(BF16)

    lane = iota((msg, 128), 1)
    row = iota((msg, 128), 0)
    base = jnp.where(
        lane == 1, place_of(ec[:msg]) * msg + (d * SLOTS).astype(F32) + rank_col[:msg],
        jnp.where(lane == 2, rg_ref[0:msg, :], 0.0),
    )
    first = jnp.where(lane == 0, tg_ref[0].astype(F32), base[0:1])
    second = jnp.where(lane == 0, tg_ref[1].astype(F32), base[1:2])
    ins[...] = jnp.where(row == 2 * d, first, jnp.where(row == 2 * d + 1, second, 0.0))
    inr[d] = ins[...]

    loads[0].wait()
    tile = min(16, rows_tok)

    def norm(i):
        at = pl.ds(pl.multiple_of(i * tile, tile), tile)
        wide = tok[at, :].astype(F32)
        mean_sq = jnp.mean(wide * wide, axis=-1, keepdims=True)
        nb[at, :] = (wide * lax.rsqrt(mean_sq + EPSILON) * gain_ref[...]).astype(BF16)

    loop(0, rows_tok // tile, norm)

    def place(ch):
        def body(k):
            values = dot(pm[ch * lanes:(ch + 1) * lanes, :], nb[:, columns(k)]).astype(BF16)
            xs[ch, 0, k] = values[:half_lanes]
            xs[ch, 1, k] = values[half_lanes:]
        loop(0, dp, body)

    def place_send(ch):
        for h in range(2):
            def body(i):
                send(xs.at[ch, h, dp_at(i)], xr.at[ch, h, d], X + 2 * ch + h, (e, dp_at(i)))
            loop(1, dp, body)
            later(xr.at[ch, h, pl.ds(0, dp - 1)], X + 2 * ch + h)
            xr[ch, h, d] = xs[ch, h, d]

    half_rows = rows // 2

    def permutations():
        a, b = iota((half_rows, half_rows), 0), iota((half_rows, half_rows), 1)
        ex, dev, slot = lax.div(a, msg), lax.rem(lax.div(a, SLOTS), dp), lax.rem(a, SLOTS)
        q[...] = jnp.where(b == dev * half_lanes + ex * SLOTS + slot, 1.0, 0.0).astype(BF16)
        ex, dev = lax.rem(lax.div(a, SLOTS), he), lax.div(a, half_lanes)
        qt[...] = jnp.where(b == ex * msg + dev * SLOTS + slot, 1.0, 0.0).astype(BF16)

    def scored_tokens(k):
        r16 = iota((msg, blk), 0)
        top = tok[0:msg, columns(k)].astype(F32)
        ts[k] = jnp.where(r16 == 2 * d, top[0:1], jnp.where(r16 == 2 * d + 1, top[1:2], 0.0)).astype(BF16)

    def dispatch(ch):
        for h in range(2):
            landed(xr.at[ch, h, pl.ds(0, dp - 1)], X + 2 * ch + h)
            moved = dot(q[...], xr[ch, h].reshape(half_rows, blk)).astype(BF16)
            zs[ch, h * he:(h + 1) * he] = moved.reshape(he, msg, blk)
            shift = lax.rem(z + h, 2)

            def body(i):
                to_y, to_z = lax.rem(y + lax.rem(i, NY), NY), lax.rem(z + 2 * lax.div(i, NY) + shift, NZ)
                at = h * he + to_y * zh + lax.div(to_z, 2)
                send(zs.at[ch, at], za.at[ch, e], Z + ch, (to_y * NZ + to_z, d))
            loop(1 - shift, he, body)
        later(za.at[ch, pl.ds(0, experts - 1)], Z + ch)
        za[ch, e] = zs[ch, place_me]

    place(0)
    permutations()
    pl.semaphore_wait(barrier, experts - 1 + dp - 1)
    place_send(0)
    place(1)
    place_send(1)
    loop(0, dp, scored_tokens)
    tr[d] = ts[d]
    dispatch(0)
    place(2)
    place_send(2)
    loop(1, dp, lambda i: send(ins, inr.at[d], IN, (e, dp_at(i))))
    loop(1, dp, lambda i: send(ts.at[dp_at(i)], tr.at[d], TS, (e, dp_at(i))))
    later(inr.at[pl.ds(0, dp - 1)], IN)
    later(tr.at[pl.ds(0, dp - 1)], TS)
    for load in loads[1:]:
        load.wait()
    dispatch(1)
    landed(inr.at[pl.ds(0, dp - 1)], IN)
    landed(tr.at[pl.ds(0, dp - 1)], TS)
    ins_total = inr[0]
    tokens16 = tr[0].astype(F32)
    for k in range(1, dp):
        ins_total = ins_total + inr[k]
        tokens16 = tokens16 + tr[k].astype(F32)
    t16[...] = tokens16
    it16[...] = ins_total
    dispatch(2)

    def gate_up(ch):
        landed(za.at[ch, pl.ds(0, experts - 1)], Z + ch)
        step = min(256, hu)

        def half(p, u):
            def body(n):
                at = pl.ds(pl.multiple_of(n * step, step), step)
                values = za[ch, pl.ds(p * he, he)].reshape(he * msg, blk)
                part[ch, u, p, :, at] = dot(values, w[u, :, at]).astype(BF16)
            loop(0, 2 * hu // step, body)

        for u in range(2):
            half(1 - c, u)
            send(part.at[ch, u, 1 - c], crecv.at[ch, u], CP + 2 * ch + u, (e, sib))
            later(crecv.at[ch, u], CP + 2 * ch + u)
        for u in range(2):
            half(c, u)
            landed(crecv.at[ch, u], CP + 2 * ch + u)

            def add(i):
                to = lax.rem(x + i, NX)
                at = pl.ds(pl.multiple_of(to * own, own), own)
                part[ch, u, c, at, :] = (
                    part[ch, u, c, at, :].astype(F32) + crecv[ch, u, at, :].astype(F32)).astype(BF16)
                return to, at

            def body(i):
                to, at = add(i)
                send(part.at[ch, u, c, at, :], xrecv.at[ch, u, i - 1], XP + 2 * ch + u, (e, 2 * to + c))
            loop(1, NX, body)
            add(0)
            later(xrecv.at[ch, u], XP + 2 * ch + u)

    def activate(ch, u):
        landed(xrecv.at[ch, u], XP + 2 * ch + u)
        at = pl.ds(pl.multiple_of(x * own, own), own)
        summed = part[ch, u, c, at, :].astype(F32)
        for i in range(NX - 1):
            summed = summed + xrecv[ch, u, i].astype(F32)
        gate, up = summed[:, :hu], summed[:, hu:]
        hid[ch, u, c, x] = (gate / (1.0 + jnp.exp(-gate)) * up).astype(BF16)
        mine = hid.at[ch, u, c, x]
        loop(1, NX, lambda i: send(mine, mine, HX + 2 * ch + u, (e, 2 * lax.rem(x + i, NX) + c)))
        later(hid.at[ch, u, 0, pl.ds(0, NX - 1)], HX + 2 * ch + u)

    def share(ch, u):
        landed(hid.at[ch, u, c, pl.ds(0, NX - 1)], HX + 2 * ch + u)
        send(hid.at[ch, u, c], hid.at[ch, u, c], HC + 2 * ch + u, (e, sib))
        later(hid.at[ch, u, 0], HC + 2 * ch + u)

    def down(ch):
        sent(Z + ch)

        def body(i):
            p = c + i - 2 * c * i

            @pl.when(i == 1)
            def _():
                for u in range(2):
                    landed(hid.at[ch, u, c], HC + 2 * ch + u)

            result = dot(hid[ch, 0, p].reshape(he * msg, hu), wd[:hu, :])
            result += dot(hid[ch, 1, p].reshape(he * msg, hu), wd[hu:, :])
            zs[ch, pl.ds(p * he, he)] = result.astype(BF16).reshape(he, msg, blk)

            def give(j):
                to = p * he + lax.rem(j + e, he)

                @pl.when(to != e)
                def _():
                    send(zs.at[ch, to], rb.at[ch, place_me], R + ch, (to, d))
            loop(0, he, give)
        loop(0, 2, body)
        rb[ch, place_me] = zs[ch, e]
        later(rb.at[ch, pl.ds(0, experts - 1)], R + ch)

    def back(ch):
        landed(rb.at[ch, pl.ds(0, experts - 1)], R + ch)

    def home(ch):
        for h in range(2):
            sent(X + 2 * ch + h)
            start = ch * lanes + h * half_lanes
            moved = dot(qt[...], rb[ch, h * he:(h + 1) * he].reshape(half_rows, blk)).astype(BF16)
            xs[ch, h] = moved.reshape(dp, half_lanes, blk)
            loop(1, dp, lambda i: send(
                xs.at[ch, h, dp_at(i)], g.at[d, pl.ds(start, half_lanes), :], T + ch, (e, dp_at(i))))
            g[d, start:start + half_lanes, :] = xs[ch, h, d]
        later(xr.at[ch, :, pl.ds(0, dp - 1)], T + ch)

    def score_rows():
        slot, scale = it16[:, 1:2], it16[:, 2:3]
        pick = jnp.where(iota((msg, rows), 1).astype(F32) == slot, 1.0, 0.0).astype(BF16)
        picked = dot(pick, rb[0].reshape(rows, blk))
        layer = (t16[...] + scale * picked).astype(BF16).astype(F32)
        fs[c, s_me, f_me, z] = (layer * fg_ref[:, columns(d)]).astype(BF16)
        mine = fs.at[c, s_me, f_me, z]
        loop(1, NZ, lambda i: send(mine, mine, FZ, (y * NZ + lax.rem(z + i, NZ), d)))
        later(fs.at[0, 0, 0, pl.ds(0, NZ - 1)], FZ)
        squares = jnp.sum(layer * layer, axis=-1, keepdims=True)
        sq[d] = jnp.broadcast_to(squares, (msg, 128))
        loop(1, dp, lambda i: send(sq.at[d], sq.at[d], SQ, (e, dp_at(i))))
        later(sq.at[pl.ds(0, dp - 1)], SQ)

    def score_info():
        landed(sq.at[pl.ds(0, dp - 1)], SQ)
        squares = sq[0]
        for k in range(1, dp):
            squares = squares + sq[k]
        info[y, z] = jnp.where(lane == 1, squares, it16[...])
        loop(1, NZ, lambda i: send(info.at[y, z], info.at[y, z], IZ, (y * NZ + lax.rem(z + i, NZ), d)))
        later(info.at[0, pl.ds(0, NZ - 1)], IZ)

    def to_y(i):
        return (lax.rem(y + i, NY) * NZ + z, d)

    def to_first(i):
        return (lax.rem(y + i * c, NY) * NZ + z, 2 * lax.rem(x + i * (1 - c), NX) + c)

    def to_second(i):
        return (lax.rem(y + i * (1 - c), NY) * NZ + z, 2 * lax.rem(x + i * c, NX) + c)

    def score_first():
        piece = fs.at[c, s_me, f_me]
        landed(fs.at[c, s_me, f_me, pl.ds(0, NZ - 1)], FZ)
        loop(1, NX, lambda i: send(piece, piece, FX, to_first(i)))
        loop(1, NX, lambda i: send(piece, piece, FYA, to_second(i)))
        later(fs.at[0, 0, pl.ds(0, NX - 1)], FX)
        later(fs.at[0, pl.ds(0, NX - 1), 0], FYA)

    def score_info_y():
        landed(info.at[y, pl.ds(0, NZ - 1)], IZ)
        loop(1, NY, lambda i: send(info.at[y], info.at[y], IY, to_y(i)))
        later(info.at[pl.ds(0, NY - 1)], IY)

    def score_second():
        landed(fs.at[c, s_me, pl.ds(0, NX - 1)], FX)

        def body(j):
            piece = fs.at[c, s_me, lax.rem(f_me + j, NX)]
            loop(1, NX, lambda i: send(piece, piece, FYB, to_second(i)))
        loop(1, NX, body)
        send(fs.at[c, s_me], fs.at[c, s_me], FC1, (e, sib))
        later(fs.at[0, pl.ds(0, NX - 1), pl.ds(0, NX - 1)], FYB)
        later(fs.at[0, 0], FC1)

    def score_core():
        landed(fs.at[c, pl.ds(0, NX - 1), 0], FYA)
        landed(fs.at[c, pl.ds(0, NX - 1), pl.ds(0, NX - 1)], FYB)

        def body(i):
            piece = fs.at[c, lax.rem(s_me + i, NX)]
            send(piece, piece, FC2, (e, sib))
        loop(1, NX, body)
        later(fs.at[0, pl.ds(0, NX - 1)], FC2)

    def logits_half(p):
        def term(i, values, core):
            acc[...] += lax.dot_general(
                un[:, columns(2 * i + core)], values.reshape(rows, blk), (((1,), (1,)), ((), ())),
                preferred_element_type=F32)

        @pl.when(p == 0)
        def _():
            loop(0, NX, lambda i: term(i, fs[0, :, i], 0))

        @pl.when(p == 1)
        def _():
            loop(0, NX, lambda i: term(i, fs[1, i], 1))

    def combine(ref, n):
        top = ref[0, 0:1]
        for k in range(1, n):
            top = jnp.maximum(top, ref[k, 0:1])
        total = jnp.zeros_like(top)
        picked = jnp.zeros_like(top)
        for k in range(n):
            total = total + ref[k, 1:2] * jnp.exp(ref[k, 0:1] - top)
            picked = picked + ref[k, 2:3]
        return top, total, picked

    def put(ref, at, stats):
        r8 = iota(ref.shape[1:], 0)
        ref[at] = jnp.where(r8 == 0, stats[0], jnp.where(r8 == 1, stats[1], jnp.where(r8 == 2, stats[2], 0.0)))

    def score_logits():
        acc[...] = jnp.zeros_like(acc)
        logits_half(c)
        landed(fs.at[c, 0], FC1)
        landed(fs.at[c, pl.ds(0, NX - 1)], FC2)
        logits_half(1 - c)
        landed(info.at[pl.ds(0, NY - 1)], IY)
        known = info[...].reshape(rows, 128).T
        target, squares = known[0:1], known[1:2]
        logits = acc[...] * lax.rsqrt(squares * (1.0 / width) + EPSILON)
        top = jnp.max(logits, axis=0, keepdims=True)
        total = jnp.sum(jnp.exp(logits - top), axis=0, keepdims=True)
        entry = iota(logits.shape, 0) + (e * dp + d) * logits.shape[0]
        picked = jnp.sum(jnp.where(entry.astype(F32) == target, logits, 0.0), axis=0, keepdims=True)
        put(stz, z, (top, total, picked))
        loop(1, NZ, lambda i: send(stz.at[z], stz.at[z], STZ, (y * NZ + lax.rem(z + i, NZ), d)))
        later(stz.at[pl.ds(0, NZ - 1)], STZ)

    def score_stats_y():
        landed(stz.at[pl.ds(0, NZ - 1)], STZ)
        put(sty, y, combine(stz, NZ))
        loop(1, NY, lambda i: send(sty.at[y], sty.at[y], STY, to_y(i)))
        later(sty.at[pl.ds(0, NY - 1)], STY)

    def score_stats_dp():
        landed(sty.at[pl.ds(0, NY - 1)], STY)
        put(std, d, combine(sty, NY))
        loop(1, dp, lambda i: send(std.at[d], std.at[d], STD, (e, dp_at(i))))
        later(std.at[pl.ds(0, dp - 1)], STD)

    def score_end():
        landed(std.at[pl.ds(0, dp - 1)], STD)
        top, total, picked = combine(std, dp)
        lp_ref[...] = picked - (top + jnp.log(total))

    def finish():
        for ch in range(CHUNKS):
            landed(g.at[pl.ds(0, dp - 1), pl.ds(0, lanes), :], T + ch)

        def body(k):
            at = columns(k)
            picked = dot(um[...], g[k])
            tok[:, at] = (tok[:, at].astype(F32) + rg_ref[...] * picked).astype(BF16)
            pltpu.make_async_copy(tok.at[:, at], out_h.at[:, at], osem).start()
        loop(0, dp, body)

    def expert(ch):
        gate_up(ch)
        for u in range(2):
            activate(ch, u)
        for u in range(2):
            share(ch, u)
        down(ch)

    expert(0)
    expert(1)
    gate_up(2)
    back(0)
    score_rows()
    home(0)
    score_info()
    score_first()
    activate(2, 0)
    activate(2, 1)
    score_info_y()
    score_second()
    share(2, 0)
    share(2, 1)
    down(2)
    back(1)
    home(1)
    score_core()
    back(2)
    home(2)
    score_logits()
    score_stats_y()
    finish()
    score_stats_dp()
    score_end()
    pltpu.make_async_copy(tok, out_h, osem).wait()

    for idx in list(pending):
        sent(idx)


def local(
    tokens, norm_gain, routing, route_gate, gate_weight, up_weight, down_weight,
    final_gain, unembed, targets,
):
    rows_tok, width = tokens.shape
    dp, experts = 2 * NX, NY * NZ
    blk, units, vocab = width // dp, up_weight.shape[2], unembed.shape[0]
    lanes, msg = experts * SLOTS, dp * SLOTS
    rows = experts * msg
    own = rows // dp
    vmem = pl.BlockSpec(memory_space=pltpu.VMEM)
    hbm = pl.BlockSpec(memory_space=pl.ANY)
    smem = pl.BlockSpec(memory_space=pltpu.SMEM)
    layer_out, log_probs = pl.pallas_call(
        kernel,
        out_shape=(
            jax.ShapeDtypeStruct((rows_tok, width), BF16),
            jax.ShapeDtypeStruct((1, rows), F32),
        ),
        in_specs=[hbm, vmem, vmem, vmem, smem, hbm, hbm, hbm, vmem, hbm],
        out_specs=(hbm, vmem),
        scratch_shapes=[
            pltpu.VMEM((rows_tok, 1), F32),
            pltpu.VMEM((rows_tok, width), BF16),
            pltpu.VMEM((rows_tok, width), BF16),
            pltpu.VMEM((2, blk, units), BF16),
            pltpu.VMEM((units, blk), BF16),
            pltpu.VMEM((vocab, width), BF16),
            pltpu.VMEM((CHUNKS * lanes, rows_tok), BF16),
            pltpu.VMEM((rows_tok, CHUNKS * lanes), BF16),
            pltpu.VMEM((rows // 2, rows // 2), BF16),
            pltpu.VMEM((rows // 2, rows // 2), BF16),
            pltpu.VMEM((CHUNKS, 2, dp, lanes // 2, blk), BF16),
            pltpu.VMEM((CHUNKS, 2, dp, lanes // 2, blk), BF16),
            pltpu.VMEM((CHUNKS, experts, msg, blk), BF16),
            pltpu.VMEM((CHUNKS, experts, msg, blk), BF16),
            pltpu.VMEM((CHUNKS, 2, 2, rows // 2, units), BF16),
            pltpu.VMEM((CHUNKS, 2, rows // 2, units), BF16),
            pltpu.VMEM((CHUNKS, 2, NX - 1, own, units), BF16),
            pltpu.VMEM((CHUNKS, 2, 2, NX, own, units // 2), BF16),
            pltpu.VMEM((CHUNKS, experts, msg, blk), BF16),
            pltpu.VMEM((dp, CHUNKS * lanes, blk), BF16),
            pltpu.VMEM((dp, msg, blk), BF16),
            pltpu.VMEM((dp, msg, blk), BF16),
            pltpu.VMEM((msg, blk), F32),
            pltpu.VMEM((msg, 128), F32),
            pltpu.VMEM((msg, 128), F32),
            pltpu.VMEM((dp, msg, 128), F32),
            pltpu.VMEM((NY, NZ, msg, 128), F32),
            pltpu.VMEM((dp, msg, 128), F32),
            pltpu.VMEM((2, NY, NX, NZ, msg, blk), BF16),
            pltpu.VMEM((vocab, rows), F32),
            pltpu.VMEM((8, rows), F32),
            pltpu.VMEM((NZ, 8, rows), F32),
            pltpu.VMEM((NY, 8, rows), F32),
            pltpu.VMEM((dp, 8, rows), F32),
            pltpu.SemaphoreType.DMA((SEMS,)),
            pltpu.SemaphoreType.DMA((SEMS,)),
            pltpu.SemaphoreType.DMA((7,)),
            pltpu.SemaphoreType.DMA,
        ],
        compiler_params=pltpu.CompilerParams(
            collective_id=0, has_side_effects=True, vmem_limit_bytes=VMEM_LIMIT
        ),
        name="routed_layer",
    )(
        tokens, norm_gain.reshape(1, width), routing.reshape(1, rows_tok),
        route_gate.reshape(1, rows_tok), targets, gate_weight, up_weight, down_weight,
        final_gain.reshape(1, width), unembed,
    )
    return layer_out, log_probs.reshape(rows)


def solution(mesh):
    placed = (
        P(("expert", "dp"), None),
        P(),
        P(("expert", "dp"), None),
        P(("expert", "dp")),
        P("expert", "dp", None),
        P("expert", "dp", None),
        P("expert", None, "dp"),
        P(),
        P(("expert", "dp"), None),
        P(("expert", "dp")),
    )
    return jax.shard_map(
        local,
        mesh=mesh,
        in_specs=placed,
        out_specs=(P(("expert", "dp"), None), P()),
        check_vma=False,
    )
```

```python
import functools

import jax
import jax.numpy as jnp
from jax import lax
from jax.experimental import pallas as pl
from jax.experimental.pallas import tpu as pltpu
from jax.sharding import PartitionSpec as P

MESH = pl.DeviceIdType.MESH
NY, NZ, NX = 4, 8, 4
EPSILON = 1e-06
CHUNKS = 3
SLOTS = 2
VMEM_LIMIT = 62 * 2**20

X, CP, XP, HX, HC = (6 * i for i in range(5))
Z, R, T = 30, 33, 36
TS, IN, FZ, SQ, IZ, IY, FX, FC1, STZ, STY, STD = range(39, 50)
FY, FC = 49, 52
SEMS = 56

F32, BF16 = jnp.float32, jnp.bfloat16


def iota(shape, dim):
    return lax.broadcasted_iota(jnp.int32, shape, dim)


def dot(a, b):
    return jnp.dot(a, b, preferred_element_type=F32)


def kernel(
    tok_h, gain_ref, rr_ref, rgr_ref, tg_ref, wg_h, wu_h, wd_h, fg_ref, un_h,
    out_h, lp_ref,
    rg_ref, tok, nb, w, wd, un, pm, um, q, qt, xs, xr, zs, za, part, crecv, xrecv, hid, rb, g,
    ts, tr, t16, it16, ins, inr, info, sq, fs, acc, st, stz, sty, std, ssem, rsem, lsem, osem,
):
    dp = 2 * NX
    experts = NY * NZ
    e, d = lax.axis_index("expert"), lax.axis_index("dp")
    y, z = lax.div(e, NZ), lax.rem(e, NZ)
    x, c = lax.div(d, 2), lax.rem(d, 2)
    sib = d + 1 - 2 * c
    rows_tok, width = tok.shape
    blk = width // dp
    half_lanes = xs.shape[3]
    lanes = 2 * half_lanes
    msg = dp * SLOTS
    rows = experts * msg
    he = experts // 2
    own = rows // dp
    units = wd.shape[0]
    hu = units // 2
    f_me, s_me = x * (1 - c) + y * c, y * (1 - c) + x * c

    def send(src, dst, idx, to):
        pltpu.make_async_remote_copy(
            src_ref=src, dst_ref=dst, send_sem=ssem.at[idx], recv_sem=rsem.at[idx],
            device_id=to, device_id_type=MESH,
        ).start()

    def landed(ref, idx):
        pltpu.make_async_copy(ref, ref, rsem.at[idx]).wait()

    pending = {}

    def later(ref, idx):
        pending[idx] = ref

    def sent(idx):
        ref = pending.pop(idx)
        pltpu.make_async_copy(ref, ref, ssem.at[idx]).wait()

    def loop(lo, hi, body):
        def step(i, carry):
            body(i)
            return carry
        lax.fori_loop(lo, hi, step, 0)

    def expert_at(i):
        dz, dy = lax.div(i, NY), lax.rem(i, NY)
        return lax.rem(y + dy, NY) * NZ + lax.rem(z + dz, NZ)

    def dp_at(i):
        return lax.rem(d + i, dp)

    def columns(k):
        return pl.ds(pl.multiple_of(k * blk, 128), blk)

    loads = [
        pltpu.make_async_copy(src, dst, lsem.at[i])
        for i, (src, dst) in enumerate([
            (tok_h, tok),
            (wg_h.at[0, :, pl.ds(0, hu)], w.at[0, :, pl.ds(0, hu)]),
            (wu_h.at[0, :, pl.ds(0, hu)], w.at[0, :, pl.ds(hu, hu)]),
            (wg_h.at[0, :, pl.ds(hu, hu)], w.at[1, :, pl.ds(0, hu)]),
            (wu_h.at[0, :, pl.ds(hu, hu)], w.at[1, :, pl.ds(hu, hu)]),
            (wd_h.at[0], wd), (un_h, un),
        ])
    ]
    for load in loads:
        load.start()
    barrier = pltpu.get_barrier_semaphore()

    def greet_dp(i):
        pl.semaphore_signal(barrier, inc=1, device_id=(e, dp_at(i)), device_id_type=MESH)

    def greet_expert(i):
        pl.semaphore_signal(barrier, inc=1, device_id=(expert_at(i), d), device_id_type=MESH)

    loop(1, experts, greet_expert)
    loop(1, dp, greet_dp)

    def column(values):
        n = values.shape[1]
        return jnp.sum(jnp.where(iota((n, n), 0) == iota((n, n), 1), values, 0.0), axis=1, keepdims=True)

    er = rr_ref[...].astype(F32)
    ec = column(er)
    rg_ref[...] = column(rgr_ref[...])
    same = ec == er
    before, after = iota(same.shape, 0), iota(same.shape, 1)
    rank_row = jnp.sum(jnp.where(same & (before < after), 1.0, 0.0), axis=0, keepdims=True)
    rank_col = jnp.sum(jnp.where(same & (after < before), 1.0, 0.0), axis=1, keepdims=True)

    def slot_of(rank, expert):
        chunk = jnp.floor(rank * (1.0 / SLOTS))
        return chunk * lanes + expert * SLOTS + (rank - chunk * SLOTS)

    pm[...] = jnp.where(iota(pm.shape, 0).astype(F32) == slot_of(rank_row, er), 1.0, 0.0).astype(BF16)
    um[...] = jnp.where(iota(um.shape, 1).astype(F32) == slot_of(rank_col, ec), 1.0, 0.0).astype(BF16)

    lane = iota((msg, 128), 1)
    row = iota((msg, 128), 0)
    base = jnp.where(
        lane == 1, ec[:msg] * msg + (d * SLOTS).astype(F32) + rank_col[:msg],
        jnp.where(lane == 2, rg_ref[0:msg, :], 0.0),
    )
    first = jnp.where(lane == 0, tg_ref[0].astype(F32), base[0:1])
    second = jnp.where(lane == 0, tg_ref[1].astype(F32), base[1:2])
    ins[...] = jnp.where(row == 2 * d, first, jnp.where(row == 2 * d + 1, second, 0.0))
    inr[d] = ins[...]

    loads[0].wait()
    tile = min(16, rows_tok)

    def norm(i):
        at = pl.ds(pl.multiple_of(i * tile, tile), tile)
        wide = tok[at, :].astype(F32)
        mean_sq = jnp.mean(wide * wide, axis=-1, keepdims=True)
        nb[at, :] = (wide * lax.rsqrt(mean_sq + EPSILON) * gain_ref[...]).astype(BF16)

    loop(0, rows_tok // tile, norm)

    def place(ch):
        for k in range(dp):
            values = dot(pm[ch * lanes:(ch + 1) * lanes, :], nb[:, k * blk:(k + 1) * blk]).astype(BF16)
            xs[ch, 0, k] = values[:half_lanes]
            xs[ch, 1, k] = values[half_lanes:]

    def place_send(ch):
        for h in range(2):
            def body(i):
                send(xs.at[ch, h, dp_at(i)], xr.at[ch, h, d], X + 2 * ch + h, (e, dp_at(i)))
            loop(1, dp, body)
            later(xr.at[ch, h, pl.ds(0, dp - 1)], X + 2 * ch + h)
            xr[ch, h, d] = xs[ch, h, d]

    half_rows = rows // 2

    def permutations():
        a, b = iota((half_rows, half_rows), 0), iota((half_rows, half_rows), 1)
        ex, dev, slot = lax.div(a, msg), lax.rem(lax.div(a, SLOTS), dp), lax.rem(a, SLOTS)
        q[...] = jnp.where(b == dev * half_lanes + ex * SLOTS + slot, 1.0, 0.0).astype(BF16)
        ex, dev = lax.rem(lax.div(a, SLOTS), he), lax.div(a, half_lanes)
        qt[...] = jnp.where(b == ex * msg + dev * SLOTS + slot, 1.0, 0.0).astype(BF16)

    def scored_tokens(k):
        r16 = iota((msg, blk), 0)
        top = tok[0:msg, columns(k)].astype(F32)
        ts[k] = jnp.where(r16 == 2 * d, top[0:1], jnp.where(r16 == 2 * d + 1, top[1:2], 0.0)).astype(BF16)

    def spread(ch, h, into, idx):
        elsewhere = lax.rem(lax.div(y, NY // 2) + h, 2)

        def body(i):
            to_y = h * (NY // 2) + lax.rem(y + lax.rem(i, NY // 2), NY // 2)
            to = to_y * NZ + lax.rem(z + lax.div(i, NY // 2), NZ)
            send(zs.at[ch, to], into.at[ch, e], idx, (to, d))
        loop(1 - elsewhere, he, body)

    def dispatch(ch):
        for h in range(2):
            landed(xr.at[ch, h, pl.ds(0, dp - 1)], X + 2 * ch + h)
            moved = dot(q[...], xr[ch, h].reshape(half_rows, blk)).astype(BF16)
            zs[ch, h * he:(h + 1) * he] = moved.reshape(he, msg, blk)
            if ch == 0 or (ch == 2 and h == 0):
                spread(ch, h, za, Z + ch)
        if ch == 1:
            loop(1, experts, lambda i: send(zs.at[ch, expert_at(i)], za.at[ch, e], Z + ch, (expert_at(i), d)))
        later(za.at[ch, pl.ds(0, experts - 1)], Z + ch)
        za[ch, e] = zs[ch, e]

    def dispatch_rest():
        spread(2, 1, za, Z + 2)

    place(0)
    permutations()
    pl.semaphore_wait(barrier, experts - 1 + dp - 1)
    place_send(0)
    place(1)
    place_send(1)
    loop(0, dp, scored_tokens)
    tr[d] = ts[d]
    dispatch(0)
    place(2)
    place_send(2)
    loop(1, dp, lambda i: send(ins, inr.at[d], IN, (e, dp_at(i))))
    loop(1, dp, lambda i: send(ts.at[dp_at(i)], tr.at[d], TS, (e, dp_at(i))))
    later(inr.at[pl.ds(0, dp - 1)], IN)
    later(tr.at[pl.ds(0, dp - 1)], TS)
    for load in loads[1:]:
        load.wait()
    dispatch(1)
    landed(inr.at[pl.ds(0, dp - 1)], IN)
    landed(tr.at[pl.ds(0, dp - 1)], TS)
    ins_total = inr[0]
    tokens16 = tr[0].astype(F32)
    for k in range(1, dp):
        ins_total = ins_total + inr[k]
        tokens16 = tokens16 + tr[k].astype(F32)
    t16[...] = tokens16
    it16[...] = ins_total
    dispatch(2)

    def gate_up(ch):
        landed(za.at[ch, pl.ds(0, experts - 1)], Z + ch)

        def half(p, u):
            values = za[ch, pl.ds(p * he, he)].reshape(he * msg, blk)
            part[ch, u, p] = dot(values, w[u]).astype(BF16)

        for u in range(2):
            half(1 - c, u)
            send(part.at[ch, u, 1 - c], crecv.at[ch, u], CP + 2 * ch + u, (e, sib))
            later(crecv.at[ch, u], CP + 2 * ch + u)
        for u in range(2):
            half(c, u)
            landed(crecv.at[ch, u], CP + 2 * ch + u)

            def add(i):
                to = lax.rem(x + i, NX)
                at = pl.ds(pl.multiple_of(to * own, own), own)
                part[ch, u, c, at, :] = (
                    part[ch, u, c, at, :].astype(F32) + crecv[ch, u, at, :].astype(F32)).astype(BF16)
                return to, at

            def body(i):
                to, at = add(i)
                send(part.at[ch, u, c, at, :], xrecv.at[ch, u, i - 1], XP + 2 * ch + u, (e, 2 * to + c))
            loop(1, NX, body)
            add(0)
            later(xrecv.at[ch, u], XP + 2 * ch + u)

    def activate(ch, u):
        landed(xrecv.at[ch, u], XP + 2 * ch + u)
        at = pl.ds(pl.multiple_of(x * own, own), own)
        summed = part[ch, u, c, at, :].astype(F32)
        for i in range(NX - 1):
            summed = summed + xrecv[ch, u, i].astype(F32)
        gate, up = summed[:, :hu], summed[:, hu:]
        hid[ch, u, c, x] = (gate / (1.0 + jnp.exp(-gate)) * up).astype(BF16)
        mine = hid.at[ch, u, c, x]
        loop(1, NX, lambda i: send(mine, mine, HX + 2 * ch + u, (e, 2 * lax.rem(x + i, NX) + c)))
        later(hid.at[ch, u, 0, pl.ds(0, NX - 1)], HX + 2 * ch + u)

    def share(ch, u):
        landed(hid.at[ch, u, c, pl.ds(0, NX - 1)], HX + 2 * ch + u)
        send(hid.at[ch, u, c], hid.at[ch, u, c], HC + 2 * ch + u, (e, sib))
        later(hid.at[ch, u, 0], HC + 2 * ch + u)

    def down(ch):
        sent(Z + ch)

        def body(i):
            p = c + i - 2 * c * i

            @pl.when(i == 1)
            def _():
                for u in range(2):
                    landed(hid.at[ch, u, c], HC + 2 * ch + u)

            result = dot(hid[ch, 0, p].reshape(he * msg, hu), wd[:hu, :])
            result += dot(hid[ch, 1, p].reshape(he * msg, hu), wd[hu:, :])
            zs[ch, pl.ds(p * he, he)] = result.astype(BF16).reshape(he, msg, blk)

            def give(j):
                to = p * he + lax.rem(j + e, he)

                @pl.when(to != e)
                def _():
                    send(zs.at[ch, to], rb.at[ch, e], R + ch, (to, d))
            loop(0, he, give)
        loop(0, 2, body)
        rb[ch, e] = zs[ch, e]
        later(rb.at[ch, pl.ds(0, experts - 1)], R + ch)

    def back(ch):
        landed(rb.at[ch, pl.ds(0, experts - 1)], R + ch)

    def home(ch):
        for h in range(2):
            sent(X + 2 * ch + h)
            start = ch * lanes + h * half_lanes
            moved = dot(qt[...], rb[ch, h * he:(h + 1) * he].reshape(half_rows, blk)).astype(BF16)
            xs[ch, h] = moved.reshape(dp, half_lanes, blk)
            loop(1, dp, lambda i: send(
                xs.at[ch, h, dp_at(i)], g.at[d, pl.ds(start, half_lanes), :], T + ch, (e, dp_at(i))))
            g[d, start:start + half_lanes, :] = xs[ch, h, d]
        later(xr.at[ch, :, pl.ds(0, dp - 1)], T + ch)

    def score_rows():
        slot, scale = it16[:, 1:2], it16[:, 2:3]
        pick = jnp.where(iota((msg, rows), 1).astype(F32) == slot, 1.0, 0.0).astype(BF16)
        picked = dot(pick, rb[0].reshape(rows, blk))
        layer = (t16[...] + scale * picked).astype(BF16).astype(F32)
        fs[c, s_me, f_me, z] = (layer * fg_ref[:, columns(d)]).astype(BF16)
        mine = fs.at[c, s_me, f_me, z]
        loop(1, NZ, lambda i: send(mine, mine, FZ, (y * NZ + lax.rem(z + i, NZ), d)))
        later(fs.at[0, 0, 0, pl.ds(0, NZ - 1)], FZ)
        squares = jnp.sum(layer * layer, axis=-1, keepdims=True)
        sq[d] = jnp.broadcast_to(squares, (msg, 128))
        loop(1, dp, lambda i: send(sq.at[d], sq.at[d], SQ, (e, dp_at(i))))
        later(sq.at[pl.ds(0, dp - 1)], SQ)

    def score_info():
        landed(sq.at[pl.ds(0, dp - 1)], SQ)
        squares = sq[0]
        for k in range(1, dp):
            squares = squares + sq[k]
        info[y, z] = jnp.where(lane == 1, squares, it16[...])
        loop(1, NZ, lambda i: send(info.at[y, z], info.at[y, z], IZ, (y * NZ + lax.rem(z + i, NZ), d)))
        later(info.at[0, pl.ds(0, NZ - 1)], IZ)

    def to_y(i):
        return (lax.rem(y + i, NY) * NZ + z, d)

    def to_first(i):
        return (lax.rem(y + i * c, NY) * NZ + z, 2 * lax.rem(x + i * (1 - c), NX) + c)

    def to_second(i):
        return (lax.rem(y + i * (1 - c), NY) * NZ + z, 2 * lax.rem(x + i * c, NX) + c)

    def score_first():
        piece = fs.at[c, s_me, f_me]
        landed(fs.at[c, s_me, f_me, pl.ds(0, NZ - 1)], FZ)
        loop(1, NX, lambda i: send(piece, piece, FX, to_first(i)))
        for i in (1, 3, 2):
            send(piece, piece, FY + i, to_second(i))
        later(fs.at[0, 0, pl.ds(0, NX - 1)], FX)

    def score_info_y():
        landed(info.at[y, pl.ds(0, NZ - 1)], IZ)
        loop(1, NY, lambda i: send(info.at[y], info.at[y], IY, to_y(i)))
        later(info.at[pl.ds(0, NY - 1)], IY)

    def score_second():
        landed(fs.at[c, s_me, pl.ds(0, NX - 1)], FX)

        for i in (1, 3, 2):
            def body(j):
                piece = fs.at[c, s_me, lax.rem(f_me + j, NX)]
                send(piece, piece, FY + i, to_second(i))
            loop(1, NX, body)
            later(fs.at[0, 0], FY + i)
        send(fs.at[c, s_me], fs.at[c, s_me], FC1, (e, sib))
        later(fs.at[0, 0], FC1)

    def score_core():
        for i in (1, 3, 2):
            piece = fs.at[c, lax.rem(s_me + NX - i, NX)]
            landed(piece, FY + i)
            send(piece, piece, FC + i, (e, sib))
            later(fs.at[0, 0], FC + i)

    def logits_half(p):
        def term(i, values, core):
            acc[...] += lax.dot_general(
                un[:, columns(2 * i + core)], values.reshape(rows, blk), (((1,), (1,)), ((), ())),
                preferred_element_type=F32)

        @pl.when(p == 0)
        def _():
            loop(0, NX, lambda i: term(i, fs[0, :, i], 0))

        @pl.when(p == 1)
        def _():
            loop(0, NX, lambda i: term(i, fs[1, i], 1))

    def combine(ref, n):
        top = ref[0, 0:1]
        for k in range(1, n):
            top = jnp.maximum(top, ref[k, 0:1])
        total = jnp.zeros_like(top)
        picked = jnp.zeros_like(top)
        for k in range(n):
            total = total + ref[k, 1:2] * jnp.exp(ref[k, 0:1] - top)
            picked = picked + ref[k, 2:3]
        return top, total, picked

    def put(ref, at, stats):
        r8 = iota(ref.shape[1:], 0)
        ref[at] = jnp.where(r8 == 0, stats[0], jnp.where(r8 == 1, stats[1], jnp.where(r8 == 2, stats[2], 0.0)))

    def score_own():
        acc[...] = jnp.zeros_like(acc)
        logits_half(c)

    def score_logits():
        landed(fs.at[c, 0], FC1)
        for i in range(1, NX):
            landed(fs.at[c, 0], FC + i)
        logits_half(1 - c)
        landed(info.at[pl.ds(0, NY - 1)], IY)
        known = info[...].reshape(rows, 128).T
        target, squares = known[0:1], known[1:2]
        logits = acc[...] * lax.rsqrt(squares * (1.0 / width) + EPSILON)
        top = jnp.max(logits, axis=0, keepdims=True)
        total = jnp.sum(jnp.exp(logits - top), axis=0, keepdims=True)
        entry = iota(logits.shape, 0) + (e * dp + d) * logits.shape[0]
        picked = jnp.sum(jnp.where(entry.astype(F32) == target, logits, 0.0), axis=0, keepdims=True)
        put(stz, z, (top, total, picked))
        loop(1, NZ, lambda i: send(stz.at[z], stz.at[z], STZ, (y * NZ + lax.rem(z + i, NZ), d)))
        later(stz.at[pl.ds(0, NZ - 1)], STZ)

    def score_stats_y():
        landed(stz.at[pl.ds(0, NZ - 1)], STZ)
        put(sty, y, combine(stz, NZ))
        loop(1, NY, lambda i: send(sty.at[y], sty.at[y], STY, to_y(i)))
        later(sty.at[pl.ds(0, NY - 1)], STY)

    def score_stats_dp():
        landed(sty.at[pl.ds(0, NY - 1)], STY)
        put(std, d, combine(sty, NY))
        loop(1, dp, lambda i: send(std.at[d], std.at[d], STD, (e, dp_at(i))))
        later(std.at[pl.ds(0, dp - 1)], STD)

    def score_end():
        landed(std.at[pl.ds(0, dp - 1)], STD)
        top, total, picked = combine(std, dp)
        lp_ref[...] = picked - (top + jnp.log(total))

    def finish():
        for ch in range(CHUNKS):
            landed(g.at[pl.ds(0, dp - 1), pl.ds(0, lanes), :], T + ch)

        def body(k):
            at = columns(k)
            picked = dot(um[...], g[k])
            tok[:, at] = (tok[:, at].astype(F32) + rg_ref[...] * picked).astype(BF16)
            pltpu.make_async_copy(tok.at[:, at], out_h.at[:, at], osem).start()
        loop(0, dp, body)

    def expert(ch):
        gate_up(ch)
        for u in range(2):
            activate(ch, u)
        for u in range(2):
            share(ch, u)
        down(ch)

    expert(0)
    dispatch_rest()
    gate_up(1)
    activate(1,0)
    activate(1,1)
    share(1,0)
    share(1,1)
    back(0)
    score_rows()
    score_info()
    home(0)
    gate_up(2)
    down(1)
    score_first()
    activate(2,0)
    activate(2,1)
    score_info_y()
    score_second()
    share(2,0)
    share(2,1)
    down(2)
    back(1)
    home(1)
    score_core()
    back(2)
    home(2)
    score_own()
    score_logits()
    finish()
    score_stats_y()
    score_stats_dp()
    score_end()
    pltpu.make_async_copy(tok, out_h, osem).wait()

    for idx in list(pending):
        sent(idx)


def local(
    tokens, norm_gain, routing, route_gate, gate_weight, up_weight, down_weight,
    final_gain, unembed, targets,
):
    rows_tok, width = tokens.shape
    dp, experts = 2 * NX, NY * NZ
    blk, units, vocab = width // dp, up_weight.shape[2], unembed.shape[0]
    lanes, msg = experts * SLOTS, dp * SLOTS
    rows = experts * msg
    own = rows // dp
    vmem = pl.BlockSpec(memory_space=pltpu.VMEM)
    hbm = pl.BlockSpec(memory_space=pl.ANY)
    smem = pl.BlockSpec(memory_space=pltpu.SMEM)
    layer_out, log_probs = pl.pallas_call(
        kernel,
        out_shape=(
            jax.ShapeDtypeStruct((rows_tok, width), BF16),
            jax.ShapeDtypeStruct((1, rows), F32),
        ),
        in_specs=[hbm, vmem, vmem, vmem, smem, hbm, hbm, hbm, vmem, hbm],
        out_specs=(hbm, vmem),
        scratch_shapes=[
            pltpu.VMEM((rows_tok, 1), F32),
            pltpu.VMEM((rows_tok, width), BF16),
            pltpu.VMEM((rows_tok, width), BF16),
            pltpu.VMEM((2, blk, units), BF16),
            pltpu.VMEM((units, blk), BF16),
            pltpu.VMEM((vocab, width), BF16),
            pltpu.VMEM((CHUNKS * lanes, rows_tok), BF16),
            pltpu.VMEM((rows_tok, CHUNKS * lanes), BF16),
            pltpu.VMEM((rows // 2, rows // 2), BF16),
            pltpu.VMEM((rows // 2, rows // 2), BF16),
            pltpu.VMEM((CHUNKS, 2, dp, lanes // 2, blk), BF16),
            pltpu.VMEM((CHUNKS, 2, dp, lanes // 2, blk), BF16),
            pltpu.VMEM((CHUNKS, experts, msg, blk), BF16),
            pltpu.VMEM((CHUNKS, experts, msg, blk), BF16),
            pltpu.VMEM((CHUNKS, 2, 2, rows // 2, units), BF16),
            pltpu.VMEM((CHUNKS, 2, rows // 2, units), BF16),
            pltpu.VMEM((CHUNKS, 2, NX - 1, own, units), BF16),
            pltpu.VMEM((CHUNKS, 2, 2, NX, own, units // 2), BF16),
            pltpu.VMEM((CHUNKS, experts, msg, blk), BF16),
            pltpu.VMEM((dp, CHUNKS * lanes, blk), BF16),
            pltpu.VMEM((dp, msg, blk), BF16),
            pltpu.VMEM((dp, msg, blk), BF16),
            pltpu.VMEM((msg, blk), F32),
            pltpu.VMEM((msg, 128), F32),
            pltpu.VMEM((msg, 128), F32),
            pltpu.VMEM((dp, msg, 128), F32),
            pltpu.VMEM((NY, NZ, msg, 128), F32),
            pltpu.VMEM((dp, msg, 128), F32),
            pltpu.VMEM((2, NY, NX, NZ, msg, blk), BF16),
            pltpu.VMEM((vocab, rows), F32),
            pltpu.VMEM((8, rows), F32),
            pltpu.VMEM((NZ, 8, rows), F32),
            pltpu.VMEM((NY, 8, rows), F32),
            pltpu.VMEM((dp, 8, rows), F32),
            pltpu.SemaphoreType.DMA((SEMS,)),
            pltpu.SemaphoreType.DMA((SEMS,)),
            pltpu.SemaphoreType.DMA((7,)),
            pltpu.SemaphoreType.DMA,
        ],
        compiler_params=pltpu.CompilerParams(
            collective_id=0, has_side_effects=True, vmem_limit_bytes=VMEM_LIMIT
        ),
        name="routed_layer",
    )(
        tokens, norm_gain.reshape(1, width), routing.reshape(1, rows_tok),
        route_gate.reshape(1, rows_tok), targets, gate_weight, up_weight, down_weight,
        final_gain.reshape(1, width), unembed,
    )
    return layer_out, log_probs.reshape(rows)


def solution(mesh):
    placed = (
        P(("expert", "dp"), None),
        P(),
        P(("expert", "dp"), None),
        P(("expert", "dp")),
        P("expert", "dp", None),
        P("expert", "dp", None),
        P("expert", None, "dp"),
        P(),
        P(("expert", "dp"), None),
        P(("expert", "dp")),
    )
    return jax.shard_map(
        local,
        mesh=mesh,
        in_specs=placed,
        out_specs=(P(("expert", "dp"), None), P()),
        check_vma=False,
    )
```
